32 devices in a mesh: dp: 16 (over z, y, x), edge: 2 (over core).
Axes of the slice: x: 2, y: 2, z: 4, core: 2. Of those that a mesh axis runs over, the one named last changes fastest.
Arguments:
- node_feat: float32 [16, 8, 1152], P('dp', 'edge'), may hold values from -6 to 6
- cotangent: float32 [16, 8, 1152], P('dp', 'edge'), may hold values from -6 to 6
- w_zero: float32 [384, 384], replicated, may hold values from -0.3125 to 0.3125
- w_one: float32 [2, 256, 256], replicated, may hold values from -0.25 to 0.25
- w_two: float32 [2, 128, 128], replicated, may hold values from -0.375 to 0.375
- edge_src: int32 [16, 256], P('dp', 'edge'), may hold values from 0 to 7
- edge_tgt: int32 [16, 256], P('dp', 'edge'), may hold values from 0 to 7
- counts: int32 [16, 2], P('dp', 'edge'), may hold values from 32 to 128, as said below
- wigner: float32 [16, 34, 256], P('dp', None, 'edge'), may hold values from -1 to 1, as said below
- radial: float32 [16, 256, 128], P('dp', 'edge'), may hold values from 0.3 to 3
Outputs:
- aggregate: float32 [16, 8, 1152], P('dp', 'edge')
- feat_grad: float32 [16, 8, 1152], P('dp', 'edge')
- grad_zero: float32 [384, 384], P('edge')
- grad_one: float32 [2, 256, 256], P(None, 'edge')
- grad_two: float32 [2, 128, 128], P(None, 'edge')
The draws below stay inside these ranges and needn't reach their ends.
Inputs may be any that keep to these rules, and one draw needn't show every extreme that they name: The first counts[g, d] edge slots of device d of batch g are used, the rest are padding; in every batch one device has all 128 slots used. `wigner`: for each edge the 9 degree-one entries and the 25 degree-two entries form the real Wigner matrices of one rotation, both orthogonal.
All inputs are finite; a program needn't handle non-finite values.
Results may differ from the reference program's by a relative error of at most 0.0003.
Values sent between devices are 32-bit elements; how exact they have to be, the bound alone decides.
A program may use at most 64 MiB of HBM per device.

```python
import math
import jax
import jax.numpy as jnp
from jax import lax

C = 128
NEIGH = 32
SHARDS = 2
GRAPHS = 16
ATOMS = 8
EDGE_DEV = 128
EDGES = 256


def draw_counts(key, part):
    key_base, key_full = jax.random.split(key)
    base = jax.random.randint(key_base, (GRAPHS, SHARDS), EDGE_DEV // 4, EDGE_DEV + 1)
    chosen = jax.random.randint(key_full, (GRAPHS, 1), 0, SHARDS)
    shard_ids = jnp.arange(SHARDS, dtype=jnp.int32)[None, :]
    return jnp.where(shard_ids == chosen, EDGE_DEV, base).astype(jnp.int32)


def draw_wigner(key, part):
    quats = jax.random.normal(key, (GRAPHS, EDGES, 4), jnp.float32)
    quats = quats / jnp.maximum(jnp.sqrt(jnp.sum(quats * quats, axis=-1, keepdims=True)), 1e-06)
    comp_w = quats[..., 0]
    comp_x = quats[..., 1]
    comp_y = quats[..., 2]
    comp_z = quats[..., 3]
    row_first = jnp.stack([1 - 2 * (comp_y * comp_y + comp_z * comp_z), 2 * (comp_x * comp_y - comp_z * comp_w), 2 * (comp_x * comp_z + comp_y * comp_w)], axis=-1)
    row_second = jnp.stack([2 * (comp_x * comp_y + comp_z * comp_w), 1 - 2 * (comp_x * comp_x + comp_z * comp_z), 2 * (comp_y * comp_z - comp_x * comp_w)], axis=-1)
    row_third = jnp.stack([2 * (comp_x * comp_z - comp_y * comp_w), 2 * (comp_y * comp_z + comp_x * comp_w), 1 - 2 * (comp_x * comp_x + comp_y * comp_y)], axis=-1)
    rotation = jnp.stack([row_first, row_second, row_third], axis=-2)
    order = jnp.array([1, 2, 0], dtype=jnp.int32)
    block_one = rotation[..., order, :][..., :, order]
    half_root = 1.0 / math.sqrt(2.0)
    sixth_root = 1.0 / math.sqrt(6.0)
    basis_list = [[[0.0, half_root, 0.0], [half_root, 0.0, 0.0], [0.0, 0.0, 0.0]], [[0.0, 0.0, 0.0], [0.0, 0.0, half_root], [0.0, half_root, 0.0]], [[-sixth_root, 0.0, 0.0], [0.0, -sixth_root, 0.0], [0.0, 0.0, 2.0 * sixth_root]], [[0.0, 0.0, half_root], [0.0, 0.0, 0.0], [half_root, 0.0, 0.0]], [[half_root, 0.0, 0.0], [0.0, -half_root, 0.0], [0.0, 0.0, 0.0]]]
    basis_arr = jnp.asarray(basis_list, dtype=jnp.float32)
    turned = jnp.einsum('geik,bkl,gejl->gebij', rotation, basis_arr, rotation)
    block_two = jnp.einsum('aij,gebij->geab', basis_arr, turned)
    joined = jnp.concatenate([block_one.reshape(GRAPHS, EDGES, 9), block_two.reshape(GRAPHS, EDGES, 25)], axis=-1)
    return jnp.transpose(joined, (0, 2, 1)).astype(jnp.float32)


def touch_ends(values, own_key, smallest, top_value):
    dims = values.shape
    spot = [jax.random.randint(jax.random.fold_in(own_key, axis), (), 0, dims[axis]) for axis in range(len(dims))]
    values = values.at[tuple(spot)].set(smallest)
    longest = dims.index(max(dims))
    spot[longest] = (spot[longest] + 1) % dims[longest]
    return values.at[tuple(spot)].set(top_value)


def shard_levels(key, extent, cuts, smallest, high):
    factor_of, own = 1.0, jax.random.fold_in(key, 6)
    for dim, parts in cuts:
        heights = jnp.exp(jax.random.uniform(jax.random.fold_in(own, dim), (parts,), jnp.float32, smallest / len(cuts), high / len(cuts)))
        factor_of = factor_of * jnp.repeat(heights, extent[dim] // parts).reshape([-1 if axis == dim else 1 for axis in range(len(extent))])
    return factor_of


def bell_draw(own_key, extent, width, limit, cuts=(), kind=jnp.bfloat16):
    result = jax.random.normal(own_key, extent, jnp.float32) * width
    if len(cuts) > 0:
        result = shard_levels(own_key, extent, cuts, -0.22, 0.18) * result
    return jnp.clip(result, min=-limit, max=limit).astype(kind)


def setup_inputs(seed: int = 0) -> dict:
    key_of = jax.random.split(jax.random.key(seed), 11)
    node_feat = bell_draw(key_of[0], (GRAPHS, ATOMS, 9 * C), 1.0, 6.0, ((0, 16), (1, 2)), jnp.float32)
    cotangent = bell_draw(key_of[1], (GRAPHS, ATOMS, 9 * C), 1.0, 6.0, ((0, 16), (1, 2)), jnp.float32)
    w_zero = bell_draw(key_of[2], (3 * C, 3 * C), (3 * C) ** -0.5, 0.3125, (), jnp.float32)
    w_one = bell_draw(key_of[3], (2, 2 * C, 2 * C), (4 * C) ** -0.5, 0.25, (), jnp.float32)
    w_two = bell_draw(key_of[4], (2, C, C), (2 * C) ** -0.5, 0.375, (), jnp.float32)
    edge_src = touch_ends(jax.random.randint(key_of[5], (GRAPHS, EDGES), 0, ATOMS), jax.random.fold_in(key_of[5], 1), 0, ATOMS - 1).astype(jnp.int32)
    edge_tgt = touch_ends(jax.random.randint(key_of[6], (GRAPHS, EDGES), 0, ATOMS), jax.random.fold_in(key_of[6], 1), 0, ATOMS - 1).astype(jnp.int32)
    counts = draw_counts(jax.random.fold_in(key_of[10], 71), 0)
    wigner = draw_wigner(jax.random.fold_in(key_of[10], 71), 0)
    radial = jnp.clip(jnp.exp(math.log(3.0) - 2.3025851 * jax.random.uniform(key_of[9], (GRAPHS, EDGES, C), jnp.float32) ** shard_levels(key_of[9], (GRAPHS, EDGES, C), ((0, 16), (1, 2)), -0.2, 0.2)), 0.3, 3.0)
    return {"node_feat": node_feat, "cotangent": cotangent, "w_zero": w_zero, "w_one": w_one, "w_two": w_two, "edge_src": edge_src, "edge_tgt": edge_tgt, "counts": counts, "wigner": wigner, "radial": radial}


PRECISE = lax.Precision.HIGHEST

def exact_dot(left, right):
    return jnp.dot(left, right, precision=PRECISE, preferred_element_type=jnp.float32)

def rotate(wigner_cols, coeffs, inverse):
    edge_count = coeffs.shape[0]
    order_one = wigner_cols[0:9].reshape(3, 3, edge_count)
    order_two = wigner_cols[9:34].reshape(5, 5, edge_count)
    pattern = 'jie,ejc->eic' if inverse else 'ije,ejc->eic'
    part_one = jnp.einsum(pattern, order_one, coeffs[:, 1:4], precision=PRECISE)
    part_two = jnp.einsum(pattern, order_two, coeffs[:, 4:9], precision=PRECISE)
    return jnp.concatenate([coeffs[:, 0:1], part_one, part_two], axis=1)

def split_orders(coeffs):
    zero_part = jnp.concatenate([coeffs[:, 0], coeffs[:, 2], coeffs[:, 6]], axis=1)
    plus_one = jnp.concatenate([coeffs[:, 3], coeffs[:, 7]], axis=1)
    minus_one = jnp.concatenate([coeffs[:, 1], coeffs[:, 5]], axis=1)
    return (zero_part, plus_one, minus_one, coeffs[:, 8], coeffs[:, 4])

def join_orders(zero_part, plus_one, minus_one, plus_two, minus_two):
    channels = plus_two.shape[1]
    pieces = [zero_part[:, :channels], minus_one[:, :channels], zero_part[:, channels:2 * channels], plus_one[:, :channels], minus_two, minus_one[:, channels:], zero_part[:, 2 * channels:], plus_one[:, channels:], plus_two]
    return jnp.stack(pieces, axis=1)

def mix_orders(rotated, weights_zero, weights_one, weights_two):
    zero_part, plus_one, minus_one, plus_two, minus_two = split_orders(rotated)
    return join_orders(exact_dot(zero_part, weights_zero), exact_dot(plus_one, weights_one[0]) - exact_dot(minus_one, weights_one[1]), exact_dot(minus_one, weights_one[0]) + exact_dot(plus_one, weights_one[1]), exact_dot(plus_two, weights_two[0]) - exact_dot(minus_two, weights_two[1]), exact_dot(minus_two, weights_two[0]) + exact_dot(plus_two, weights_two[1]))

def graph_forward(features, weights_zero, weights_one, weights_two, sources, targets, wigner_cols, radial_rows, edge_weight):
    atom_total = features.shape[0]
    channels = radial_rows.shape[1]
    edge_in = features.reshape(atom_total, 9, channels)[sources] * radial_rows[:, None, :]
    rotated = rotate(wigner_cols, edge_in, False)
    mixed = mix_orders(rotated, weights_zero, weights_one, weights_two)
    message = rotate(wigner_cols, mixed, True) * edge_weight[:, None, None]
    return jax.ops.segment_sum(message.reshape(-1, 9 * channels), targets, num_segments=atom_total)

def reference(node_feat, cotangent, w_zero, w_one, w_two, edge_src, edge_tgt, counts, wigner, radial):
    positions = jnp.arange(EDGES, dtype=jnp.int32)
    grad_scale = 1.0 / math.sqrt(GRAPHS * EDGES)

    def one_graph(running, graph_index):
        used_slots = counts[graph_index][positions // EDGE_DEV]
        edge_weight = jnp.where(positions % EDGE_DEV < used_slots, 1.0, 0.0).astype(jnp.float32) / math.sqrt(NEIGH)

        def forward(features, weights_zero, weights_one, weights_two):
            return graph_forward(features, weights_zero, weights_one, weights_two, edge_src[graph_index], edge_tgt[graph_index], wigner[graph_index], radial[graph_index], edge_weight)
        summed, pullback = jax.vjp(forward, node_feat[graph_index], w_zero, w_one, w_two)
        grad_feat, grad_wzero, grad_wone, grad_wtwo = pullback(cotangent[graph_index])
        return ((running[0] + grad_wzero, running[1] + grad_wone, running[2] + grad_wtwo), (summed, grad_feat))
    zeros_init = (jnp.zeros(w_zero.shape, jnp.float32), jnp.zeros(w_one.shape, jnp.float32), jnp.zeros(w_two.shape, jnp.float32))
    grad_sums, outputs = lax.scan(one_graph, zeros_init, jnp.arange(GRAPHS, dtype=jnp.int32))
    return (outputs[0], outputs[1], grad_sums[0] * grad_scale, grad_sums[1] * grad_scale, grad_sums[2] * grad_scale)
```

```python
import functools
import math

import jax
import jax.numpy as jnp
from jax import lax
from jax.experimental import pallas as pl
from jax.experimental.pallas import tpu as pltpu
from jax.sharding import PartitionSpec as P

NEIGH = 32
PLACE = (0, 2, 6, 3, 7, 1, 5, 8, 4)
SPOT = tuple(PLACE.index(k) for k in range(9))
MESH = pl.DeviceIdType.MESH
F32 = jnp.float32
B16 = jnp.bfloat16


def digits(count):
    steps = []
    stride = 1
    while stride < count:
        left = count // stride
        radix = 2 if len(steps) < 2 or left < 4 else 4
        steps.append((stride, radix))
        stride *= radix
    assert stride == count
    return steps


def split(x):
    hi = x.astype(B16)
    return hi, (x - hi.astype(F32)).astype(B16)


def dot(a, b, dims=((1,), (0,))):
    return lax.dot_general(a, b, (dims, ((), ())), preferred_element_type=F32)


def dot3(a, b, dims=((1,), (0,))):
    return dot(a[0], b[0], dims) + dot(a[0], b[1], dims) + dot(a[1], b[0], dims)


def plan(dp, shards, ch):
    rz, r1, r2 = 3 * ch // shards, 2 * ch // shards, ch // shards
    valid = (3 * rz + r2, 4 * r1 + r2)
    unit = 8 * dp
    padded = tuple(-(-v // unit) * unit for v in valid)
    steps = digits(dp)
    ahead = list(range(len(steps)))
    swapped = ahead[:2][::-1] + ahead[2:]
    pieces = []
    offset = 0
    for half, rows in enumerate(padded):
        units = rows // unit
        first = (units + 1) // 2
        orders = (ahead, swapped) if half == 0 else (swapped, ahead)
        for size, order in zip((first, units - first), orders):
            if size:
                pieces.append((half, offset, size * unit, order))
                offset += size * unit
    return (rz, r1, r2), valid, padded, steps, pieces


def kernel(
    dp, shards, laid,
    feat_ref, cot_ref, src_ref, tgt_ref, counts_ref, wig_ref, rad_ref, w0_hbm, w1_hbm, w2_hbm,
    agg_ref, fg_ref, g0_ref, g1_ref, g2_ref,
    w0_f, w1_f, w2_f, w0_s, w1_s, w2_s,
    feats, cots, efeat, ecot, wig_t, wb, rot, gmx, mixed, rot_t3, g3,
    esend, erecv, acc, gat, rbuf,
    aggs, aggr, fgs, fgr,
    wsem, fsend, frecv, esnd, ercv, psend, precv, asend, arecv,
):
    (rz, r1, r2), valid, padded, steps, pieces = laid
    edges, ch = rad_ref.shape[1], rad_ref.shape[2]
    atom_dev = feat_ref.shape[1]
    atoms = atom_dev * shards
    apad = -(-atoms // 16) * 16
    wide = 9 * ch
    me_d, me_e = lax.axis_index("dp"), lax.axis_index("edge")
    half_off = (0, padded[0])
    z0, p1, n1, p2, n2 = 0, 3 * ch, 5 * ch, 7 * ch, 8 * ch

    def peer_edge(k):
        return lax.rem(me_e + k, shards)

    def digit(step):
        stride, radix = steps[step]
        return lax.rem(me_d // stride, radix)

    def partner(step, k):
        stride, radix = steps[step]
        mine = digit(step)
        other = lax.rem(mine + k, radix)
        return other, me_d + (other - mine) * stride

    barrier = pltpu.get_barrier_semaphore()
    greeted = 0
    for k in range(1, shards):
        pl.semaphore_signal(barrier, inc=1, device_id=(me_d, peer_edge(k)), device_id_type=MESH)
        greeted += 1
    for step in range(len(steps)):
        for k in range(1, steps[step][1]):
            pl.semaphore_signal(
                barrier, inc=1, device_id=(partner(step, k)[1], me_e), device_id_type=MESH
            )
            greeted += 1

    loads = [
        pltpu.make_async_copy(src, dst, wsem.at[i])
        for i, (src, dst) in enumerate(((w0_hbm, w0_f), (w1_hbm, w1_f), (w2_hbm, w2_f)))
    ]
    for load in loads:
        load.start()

    count = counts_ref[0, 0]
    atom_ids = lax.broadcasted_iota(jnp.int32, (apad, edges), 0)
    slots = lax.broadcasted_iota(jnp.int32, (apad, edges), 1)
    src_hot = jnp.where(atom_ids == src_ref[...], 1.0, 0.0).astype(F32)
    tgt_hot = jnp.where((atom_ids == tgt_ref[...]) & (slots < count), 1.0, 0.0).astype(F32)
    src_cols = jnp.concatenate([src_hot, src_hot], axis=0).T.astype(B16)
    tgt_cols = jnp.concatenate([tgt_hot, tgt_hot], axis=0).T.astype(B16)
    src_rows = jnp.concatenate([src_hot, src_hot], axis=1).astype(B16)
    tgt_rows = jnp.concatenate([tgt_hot, tgt_hot], axis=1).astype(B16)
    wig = jnp.concatenate([wig_ref[0], jnp.zeros((ch - 34, edges), F32)], axis=0)
    wig_t[...] = wig.T
    for half in range(2):
        spare = padded[half] - valid[half]
        if spare:
            acc[half_off[half] + valid[half] : half_off[half] + padded[half], :] = jnp.zeros(
                (spare, ch), F32
            )

    pl.semaphore_wait(barrier, greeted)

    copies = []
    for k in range(1, shards):
        for j, (mine, gathered) in enumerate(((feat_ref, feats), (cot_ref, cots))):
            copy = pltpu.make_async_remote_copy(
                src_ref=mine.at[0],
                dst_ref=gathered.at[me_e],
                send_sem=fsend.at[2 * (k - 1) + j],
                recv_sem=frecv.at[2 * (k - 1) + j],
                device_id=(me_d, peer_edge(k)),
                device_id_type=MESH,
            )
            copy.start()
            copies.append(copy)
    feats[me_e] = feat_ref[0]
    cots[me_e] = cot_ref[0]

    def spread(i, carry):
        rows = pl.ds(pl.multiple_of(i * 8, 8), 8)
        cols = wig_t[rows, :]
        for k in range(34):
            wb[k, rows, :] = jnp.broadcast_to(cols[:, k : k + 1], (8, ch))
        return carry

    lax.fori_loop(0, edges // 8, spread, 0)

    for copy in copies:
        copy.wait()

    def stacked(gathered, factor):
        parts = [gathered[s] for s in range(shards)]
        if apad > atoms:
            parts.append(jnp.zeros((apad - atoms, wide), F32))
        whole = jnp.concatenate(parts, axis=0) * factor
        hi = whole.astype(B16).astype(F32)
        return jnp.concatenate([hi, whole - hi], axis=0).astype(B16)

    norm = 1.0 / math.sqrt(NEIGH)
    efeat[...] = dot(src_cols, stacked(feats, 1.0))
    ecot[...] = dot(tgt_cols, stacked(cots, norm))

    def turn(w, x, inverse):
        out = [x[0]]
        for first, size, base in ((1, 3, 0), (4, 5, 9)):
            for i in range(size):
                total = None
                for j in range(size):
                    entry = base + (size * j + i if inverse else size * i + j)
                    term = w[entry] * x[first + j]
                    total = term if total is None else total + term
                out.append(total)
        return out

    def rotate_in(i, carry):
        rows = pl.ds(pl.multiple_of(i * 8, 8), 8)
        w = [wb[k, rows, :] for k in range(34)]
        radial = rad_ref[0, rows, :]
        x = [efeat[rows, k * ch : (k + 1) * ch] * radial for k in range(9)]
        for k, value in enumerate(turn(w, x, False)):
            rot[rows, SPOT[k] * ch : (SPOT[k] + 1) * ch] = value
        x = [ecot[rows, k * ch : (k + 1) * ch] for k in range(9)]
        for k, value in enumerate(turn(w, x, False)):
            gmx[rows, SPOT[k] * ch : (SPOT[k] + 1) * ch] = value
        return carry

    lax.fori_loop(0, edges // 8, rotate_in, 0)

    for b in range(9):
        cols = slice(b * ch, (b + 1) * ch)
        hi, lo = split(rot[:, cols].T)
        rot_t3[cols, 0:edges] = hi
        rot_t3[cols, edges : 2 * edges] = hi
        rot_t3[cols, 2 * edges :] = lo
        hi, lo = split(gmx[:, cols])
        g3[0:edges, cols] = hi
        g3[edges : 2 * edges, cols] = lo
        g3[2 * edges :, cols] = hi

    def lhs(start, size, owner):
        return rot_t3[pl.ds(pl.multiple_of(start + owner * size, 16), size), :]

    def share_a(owner, out):
        zero = dot(lhs(z0, rz, owner), g3[:, z0:p1])
        for b in range(3):
            out[b * rz : (b + 1) * rz, :] = zero[:, b * ch : (b + 1) * ch]
        out[3 * rz : 3 * rz + r2, :] = dot(lhs(p2, r2, owner), g3[:, p2:n2]) + dot(
            lhs(n2, r2, owner), g3[:, n2:]
        )

    def share_b(owner, out):
        plus, minus = lhs(p1, r1, owner), lhs(n1, r1, owner)
        gp, gn = g3[:, p1:n1], g3[:, n1:p2]
        real = dot(plus, gp) + dot(minus, gn)
        imag = dot(plus, gn) - dot(minus, gp)
        for b in range(2):
            out[b * r1 : (b + 1) * r1, :] = real[:, b * ch : (b + 1) * ch]
            out[(2 + b) * r1 : (3 + b) * r1, :] = imag[:, b * ch : (b + 1) * ch]
        out[4 * r1 : 4 * r1 + r2, :] = dot(lhs(p2, r2, owner), g3[:, n2:]) - dot(
            lhs(n2, r2, owner), g3[:, p2:n2]
        )

    shares = (share_a, share_b)
    ecopies = [[], []]
    for half in range(2):
        for k in range(1, shards):
            span = pl.ds(half_off[half], valid[half])
            shares[half](peer_edge(k), esend.at[k - 1, span])
            copy = pltpu.make_async_remote_copy(
                src_ref=esend.at[k - 1, span],
                dst_ref=erecv.at[k - 1, span],
                send_sem=esnd.at[2 * (k - 1) + half],
                recv_sem=ercv.at[2 * (k - 1) + half],
                device_id=(me_d, peer_edge(k)),
                device_id_type=MESH,
            )
            copy.start()
            ecopies[half].append(copy)

    grad_scale = 1.0 / math.sqrt(dp * shards * edges)
    slots_used = [0, 0]
    jobs = []

    class Piece:
        pass

    for half, offset, length, order in pieces:
        piece = Piece()
        piece.half, piece.order, piece.at, piece.len = half, order, offset, length
        piece.base = jnp.int32(0) + offset
        piece.trail = []
        piece.pending = None
        piece.every = []
        jobs.append(piece)

    def send_to(src, dst, target):
        sem = slots_used[0]
        slots_used[0] += 1
        copy = pltpu.make_async_remote_copy(
            src_ref=src, dst_ref=dst, send_sem=psend.at[sem], recv_sem=precv.at[sem],
            device_id=(target, me_e), device_id_type=MESH,
        )
        copy.start()
        return copy

    def start_scatter(piece, n):
        step = piece.order[n]
        part = piece.len // steps[step][1]
        piece.pending = []
        for k in range(1, steps[step][1]):
            other, target = partner(step, k)
            begin = pl.multiple_of(piece.base + other * part, 8)
            slot = pl.ds(slots_used[1], part)
            slots_used[1] += part
            copy = send_to(acc.at[pl.ds(begin, part)], rbuf.at[slot], target)
            piece.pending.append((copy, slot))

    def end_scatter(piece, n):
        step = piece.order[n]
        part = piece.len // steps[step][1]
        piece.trail.append((piece.base, piece.len))
        piece.base = piece.base + digit(step) * part
        piece.len = part
        own = pl.ds(pl.multiple_of(piece.base, 8), part)
        total = acc[own, :]
        for copy, slot in piece.pending:
            copy.wait_recv()
            piece.every.append(copy)
            total = total + rbuf[slot, :]
        if n == len(steps) - 1:
            gat[own, :] = total * grad_scale
        else:
            acc[own, :] = total

    def start_gather(piece, n):
        step = piece.order[n]
        own = pl.ds(pl.multiple_of(piece.base, 8), piece.len)
        piece.pending = [
            send_to(gat.at[own], gat.at[own], partner(step, k)[1])
            for k in range(1, steps[step][1])
        ]

    def end_gather(piece, n):
        for copy in piece.pending:
            copy.wait_recv()
            piece.every.append(copy)
        piece.base, piece.len = piece.trail.pop()

    last = len(steps) - 1
    if dp == 1:
        jobs = []

    for half in range(2):
        span = pl.ds(half_off[half], valid[half])
        shares[half](me_e, acc.at[span])
        total = acc[span, :]
        for k, copy in enumerate(ecopies[half]):
            copy.wait_recv()
            total = total + erecv[k, span, :]
        acc[span, :] = total
        for piece in jobs:
            if piece.half == half:
                start_scatter(piece, 0)

    eye = ((1,), (0,))
    flip = ((1,), (1,))

    def mix(hi, lo, out, sign, dims):
        zero = dot3((hi[:, z0:p1], lo[:, z0:p1]), (w0_s[0], w0_s[1]), dims)
        out[:, z0:p1] = zero
        for begin, middle, end, weights in ((p1, n1, p2, w1_s), (p2, n2, wide, w2_s)):
            pair = tuple(
                jnp.concatenate([v[:, begin:middle], v[:, middle:end]], axis=0) for v in (hi, lo)
            )
            real = dot3(pair, (weights[0, 0], weights[1, 0]), dims)
            imag = dot3(pair, (weights[0, 1], weights[1, 1]), dims)
            if sign > 0:
                out[:, begin:middle] = real[:edges] - imag[edges:]
                out[:, middle:end] = real[edges:] + imag[:edges]
            else:
                out[:, begin:middle] = real[:edges] + imag[edges:]
                out[:, middle:end] = real[edges:] - imag[:edges]

    def rotate_out(dest, use_radial):
        def body(i, carry):
            rows = pl.ds(pl.multiple_of(i * 8, 8), 8)
            w = [wb[k, rows, :] for k in range(34)]
            x = [mixed[rows, SPOT[k] * ch : (SPOT[k] + 1) * ch] for k in range(9)]
            for k, value in enumerate(turn(w, x, True)):
                if use_radial:
                    value = value * rad_ref[0, rows, :]
                dest[rows, k * ch : (k + 1) * ch] = value
            return carry

        lax.fori_loop(0, edges // 8, body, 0)

    def collect(hot, values, factor, sent, received, sem):
        hi, lo = split(values[...])
        total = dot(hot, jnp.concatenate([hi, lo], axis=0)) * factor
        for s in range(shards):
            sent[s] = total[s * atom_dev : (s + 1) * atom_dev]
        started = []
        for k in range(1, shards):
            copy = pltpu.make_async_remote_copy(
                src_ref=sent.at[peer_edge(k)],
                dst_ref=received.at[k - 1],
                send_sem=asend.at[2 * (k - 1) + sem],
                recv_sem=arecv.at[2 * (k - 1) + sem],
                device_id=(me_d, peer_edge(k)),
                device_id_type=MESH,
            )
            copy.start()
            started.append(copy)
        return started

    tail = {}

    def forward_mix():
        for load in loads:
            load.wait()
        hi, lo = split(w0_f[...])
        w0_s[0], w0_s[1] = hi, lo
        hi, lo = split(w1_f[...])
        w1_s[0], w1_s[1] = hi, lo
        hi, lo = split(w2_f[...])
        w2_s[0], w2_s[1] = hi, lo
        hi, lo = split(rot[...])
        mix(hi, lo, mixed, 1, eye)

    def forward_rest():
        rotate_out(efeat, False)
        tail["agg"] = collect(tgt_rows, efeat, norm, aggs, aggr, 0)

    def backward_mix():
        mix(g3[0:edges, :], g3[edges : 2 * edges, :], mixed, -1, flip)

    def backward_rest():
        rotate_out(ecot, True)
        tail["fg"] = collect(src_rows, ecot, 1.0, fgs, fgr, 1)

    def finish_rows():
        for name, out, sent, received in (("agg", agg_ref, aggs, aggr), ("fg", fg_ref, fgs, fgr)):
            total = sent[me_e]
            for k, copy in enumerate(tail[name]):
                copy.wait()
                total = total + received[k]
            out[0] = total

    work = [forward_mix, forward_rest, backward_mix, backward_rest, finish_rows]

    for n in range(len(steps)):
        if work:
            work.pop(0)()
        for piece in jobs:
            end_scatter(piece, n)
            if n < last:
                start_scatter(piece, n + 1)
            else:
                start_gather(piece, n)
    for n in reversed(range(len(steps))):
        if work:
            work.pop(0)()
        for piece in jobs:
            end_gather(piece, n)
            if n > 0:
                start_gather(piece, n - 1)
    while work:
        work.pop(0)()
    for half in range(2):
        for copy in ecopies[half]:
            copy.wait_send()
    for piece in jobs:
        for copy in piece.every:
            copy.wait_send()

    source = gat if dp > 1 else acc
    factor = 1.0 if dp > 1 else grad_scale

    def block(begin, size):
        value = source[begin : begin + size, :]
        return value if dp > 1 else value * factor

    for b in range(3):
        g0_ref[:, b * ch : (b + 1) * ch] = block(b * rz, rz)
    g2_ref[0] = block(3 * rz, r2)
    for part in range(2):
        for b in range(2):
            g1_ref[part, :, b * ch : (b + 1) * ch] = block(half_off[1] + (2 * part + b) * r1, r1)
    g2_ref[1] = block(half_off[1] + 4 * r1, r2)


def local(dp, shards, node_feat, cotangent, w_zero, w_one, w_two, edge_src, edge_tgt, counts, wigner, radial):
    atom_dev = node_feat.shape[1]
    edges, ch = radial.shape[1], radial.shape[2]
    wide = 9 * ch
    laid = plan(dp, shards, ch)
    (rz, r1, r2), valid, padded, steps, pieces = laid
    rows = sum(padded)
    copies = 0
    landing = 0
    for _, _, length, order in pieces:
        for n in order:
            radix = steps[n][1]
            copies += 2 * (radix - 1)
            length //= radix
            landing += length * (radix - 1)
    peers = max(shards - 1, 1)
    vmem = pl.BlockSpec(memory_space=pltpu.VMEM)
    smem = pl.BlockSpec(memory_space=pltpu.SMEM)
    anywhere = pl.BlockSpec(memory_space=pl.ANY)
    dma = pltpu.SemaphoreType.DMA
    return pl.pallas_call(
        functools.partial(kernel, dp, shards, laid),
        out_shape=(
            jax.ShapeDtypeStruct((1, atom_dev, wide), F32),
            jax.ShapeDtypeStruct((1, atom_dev, wide), F32),
            jax.ShapeDtypeStruct((rz, 3 * ch), F32),
            jax.ShapeDtypeStruct((2, r1, 2 * ch), F32),
            jax.ShapeDtypeStruct((2, r2, ch), F32),
        ),
        in_specs=[vmem, vmem, vmem, vmem, smem, vmem, vmem, anywhere, anywhere, anywhere],
        out_specs=(vmem,) * 5,
        scratch_shapes=[
            pltpu.VMEM(w_zero.shape, F32),
            pltpu.VMEM(w_one.shape, F32),
            pltpu.VMEM(w_two.shape, F32),
            pltpu.VMEM((2,) + w_zero.shape, B16),
            pltpu.VMEM((2,) + w_one.shape, B16),
            pltpu.VMEM((2,) + w_two.shape, B16),
            pltpu.VMEM((shards, atom_dev, wide), F32),
            pltpu.VMEM((shards, atom_dev, wide), F32),
            pltpu.VMEM((edges, wide), F32),
            pltpu.VMEM((edges, wide), F32),
            pltpu.VMEM((edges, ch), F32),
            pltpu.VMEM((34, edges, ch), F32),
            pltpu.VMEM((edges, wide), F32),
            pltpu.VMEM((edges, wide), F32),
            pltpu.VMEM((edges, wide), F32),
            pltpu.VMEM((wide, 3 * edges), B16),
            pltpu.VMEM((3 * edges, wide), B16),
            pltpu.VMEM((peers, rows, ch), F32),
            pltpu.VMEM((peers, rows, ch), F32),
            pltpu.VMEM((rows, ch), F32),
            pltpu.VMEM((rows, ch), F32),
            pltpu.VMEM((max(landing, 8), ch), F32),
            pltpu.VMEM((shards, atom_dev, wide), F32),
            pltpu.VMEM((peers, atom_dev, wide), F32),
            pltpu.VMEM((shards, atom_dev, wide), F32),
            pltpu.VMEM((peers, atom_dev, wide), F32),
            dma((3,)),
            dma((2 * peers,)),
            dma((2 * peers,)),
            dma((2 * peers,)),
            dma((2 * peers,)),
            dma((max(copies, 1),)),
            dma((max(copies, 1),)),
            dma((2 * peers,)),
            dma((2 * peers,)),
        ],
        compiler_params=pltpu.CompilerParams(
            collective_id=0, has_side_effects=True, vmem_limit_bytes=40 * 1024 * 1024
        ),
    )(node_feat, cotangent, edge_src, edge_tgt, counts, wigner, radial, w_zero, w_one, w_two)


def solution(mesh):
    placed = (
        P("dp", "edge", None),
        P("dp", "edge", None),
        P(),
        P(),
        P(),
        P("dp", "edge"),
        P("dp", "edge"),
        P("dp", "edge"),
        P("dp", None, "edge"),
        P("dp", "edge", None),
    )
    return jax.shard_map(
        functools.partial(local, mesh.shape["dp"], mesh.shape["edge"]),
        mesh=mesh,
        in_specs=placed,
        out_specs=(
            P("dp", "edge", None),
            P("dp", "edge", None),
            P("edge", None),
            P(None, "edge", None),
            P(None, "edge", None),
        ),
        check_vma=False,
    )
```
